512 devices in a mesh: expert: 64 (over x, y, core), seq: 8 (over z).
Axes of the slice: x: 4, y: 8, z: 8, core: 2. Of those that a mesh axis runs over, the one named last changes fastest.
Arguments:
- hidden_rows: bfloat16 [32768, 8, 1024], P(('expert', 'seq')), may hold values from -16 to 16
- routes: int32 [32768, 8], P(('expert', 'seq')), may hold values from 0 to 63, all different within a row; in each aligned block of 64 rows (0 to 63, 64 to 127, ...) at most 16 rows name the same one
- down_weight: bfloat16 [64, 7168, 1024], P('expert', 'seq'), may hold values from -0.1875 to 0.1875
- probe: bfloat16 [7168, 256], P('seq'), may hold values from -0.0625 to 0.0625
Outputs:
- basis: float32 [7168, 256], P(('seq', 'expert'))
- coefficients: float32 [64, 256, 1024], P('expert', None, 'seq')
The draws below stay inside these ranges and needn't reach their ends.
Inputs may be any that keep to these rules, and one draw needn't show every extreme that they name: `routes`: in each aligned block of 64 tokens no expert is named in more than 16 places, and some expert in exactly 16; the 8 experts of a token differ.
All inputs are finite; a program needn't handle non-finite values.
Results may differ from the reference program's by a relative error of at most 0.0054.
Values may be sent and summed in bfloat16 or wider, within the bound.
No kernel may reach another device: no remote copies, remote signals or barrier semaphores. Data moves between devices by JAX's collectives and lax.ppermute only.
A program may use at most 64 MiB of HBM per device.

```python
import math
import jax
import jax.numpy as jnp
import numpy as np
from jax import lax

D = 7168
FF = 1024
TOP = 8
P_SIZE = 256
TOK_DEV = 64
EXPERTS = 64
TOKENS = 32768
CAP = 16
ROW_MEAN = 4096


def draw_hidden_rows(key, part):
    key = jax.random.fold_in(key, 7)
    base_key, column_key, row_key = jax.random.split(key, 3)
    column_scale = jnp.exp(jax.random.uniform(column_key, (FF,), jnp.float32, math.log(0.3), math.log(3.0)))
    row_scale = jnp.exp(jax.random.uniform(row_key, (TOKENS, TOP, 1), jnp.float32, math.log(0.5), math.log(2.0)))
    values = jax.random.normal(base_key, (TOKENS, TOP, FF), jnp.float32)
    return jnp.clip(values * column_scale * row_scale, -16.0, 16.0).astype(jnp.bfloat16)


def shard_levels(key, shape, pieces, low, high):
    gain, own = 1.0, jax.random.fold_in(key, 6)
    for axis_at, blocks in pieces:
        draws = jnp.exp(jax.random.uniform(jax.random.fold_in(own, axis_at), (blocks,), jnp.float32, low / len(pieces), high / len(pieces)))
        gain = gain * jnp.repeat(draws, shape[axis_at] // blocks).reshape([-1 if axis == axis_at else 1 for axis in range(len(shape))])
    return gain


def shared_out(rng, own, number, rows, amount, top, bound, skew):
    order = jax.random.permutation(rng, amount)
    heavy_load, ordinary = load_shares(amount, rows * top, bound, skew, True), load_shares(amount, rows * top, bound, skew, False)
    places = jnp.arange(amount)

    def named(lengths, turn):
        used = int((lengths > 0).sum())
        fixed = max(1, used // 4)
        passed = fixed + (places - fixed + turn * (used - fixed)) % max(1, amount - fixed)
        return jnp.zeros((amount,), jnp.int32).at[order[jnp.where(places < fixed, places, passed)]].set(jnp.asarray(lengths, jnp.int32))

    lengths = jnp.where(number % 4 == 0, named(heavy_load, number // 4), named(ordinary, number - number // 4 - 1))
    mixed = jax.random.permutation(jax.random.fold_in(own, 3), amount)
    giver, taker = mixed[0:amount // 2 * 2:2], mixed[1:amount // 2 * 2:2]
    slack = jnp.minimum(lengths[giver] - 1, bound - lengths[taker]) // 2
    slack = jnp.where((giver == order[0]) | (taker == order[0]) | (lengths[taker] == 0), 0, jnp.maximum(slack, 0))
    passed = jax.random.randint(jax.random.fold_in(own, 4), (amount // 2,), 0, 1 << 20) % (slack + 1)
    lengths = lengths.at[giver].add(-passed).at[taker].add(passed)
    members = jnp.searchsorted(jnp.cumsum(lengths), jnp.arange(rows * top), side="right").astype(jnp.int32)
    table = members.reshape(top, rows).T
    table = table[jax.random.permutation(jax.random.fold_in(own, 1), rows)]
    turn = jax.random.randint(jax.random.fold_in(own, 2), (rows, 1), 0, top)
    return jnp.take_along_axis(table, (jnp.arange(top)[None, :] + turn) % top, axis=1)


def load_shares(count, total, bound, lean, full):
    portions = [(1 << 20) // math.isqrt(rank ** lean) + 1 for rank in range(1, count + 1)]
    largest = bound if full else min(bound, max(-(-total // count), total * portions[0] // sum(portions)))
    least = 1 if total - largest >= count - 1 else 0
    given, spare = [largest] + [least] * (count - 1), total - largest - least * (count - 1)
    while spare > 0:
        free = [i for i in range(1, count) if given[i] < largest] or [i for i in range(1, count) if given[i] < bound]
        pool, remaining = sum([portions[i] for i in free]), spare
        for i in free:
            extra = min(bound - given[i], max(1, remaining * portions[i] // pool), spare)
            given[i] = given[i] + extra
            spare = spare - extra
    return np.array(given)


def noise(stream_key, shape, width, limit, cuts=(), held_as=jnp.bfloat16):
    drawn = width * jax.random.normal(stream_key, shape, jnp.float32)
    if cuts:
        drawn = drawn * shard_levels(stream_key, shape, cuts, -0.22, 0.18)
    return jnp.clip(drawn, -limit, limit).astype(held_as)


def setup_inputs(seed: int = 0) -> dict:
    key_list = jax.random.split(jax.random.key(seed), 5)
    hidden_rows = draw_hidden_rows(jax.random.fold_in(key_list[4], 71), 0)
    routes_keys = jax.random.split(jax.random.fold_in(key_list[1], 1), TOKENS // TOK_DEV)
    routes_turns = jax.random.permutation(jax.random.fold_in(key_list[1], 3), TOKENS // TOK_DEV)
    routes = jax.vmap(lambda own, number: shared_out(jax.random.fold_in(key_list[1], 2), own, number, TOK_DEV, EXPERTS, TOP, CAP, 2))(routes_keys, routes_turns).reshape((TOKENS, TOP))
    down_weight = noise(key_list[2], (EXPERTS, D, FF), FF ** -0.5, 0.1875, ((0, 64), (1, 8)))
    probe = noise(key_list[3], (D, P_SIZE), D ** -0.5, 0.0625, ((0, 8),))
    return {"hidden_rows": hidden_rows, "routes": routes, "down_weight": down_weight, "probe": probe}


def reference(hidden_rows, routes, down_weight, probe):
    flat_rows = hidden_rows.reshape(-1, FF)
    expert_ids = routes.reshape(-1).astype(jnp.int32)
    row_limit = (TOKENS // TOK_DEV) * CAP
    row_order = jnp.argsort(expert_ids, stable=True).astype(jnp.int32)
    row_order = jnp.concatenate([row_order, jnp.zeros((row_limit,), jnp.int32)])
    labels = jnp.arange(EXPERTS, dtype=jnp.int32)
    counts = jnp.sum((expert_ids[:, None] == labels[None, :]).astype(jnp.int32), axis=0).astype(jnp.int32)
    starts = (jnp.cumsum(counts) - counts).astype(jnp.int32)

    def expert_panel(running, inputs):
        weight, first, count = inputs
        probe_proj = lax.dot_general(weight, probe, (((0,), (0,)), ((), ())), preferred_element_type=jnp.float32).astype(jnp.bfloat16)
        picked = lax.dynamic_slice(row_order, (first.astype(jnp.int32),), (row_limit,))
        live_mask = jnp.arange(row_limit, dtype=jnp.int32) < count
        chosen_rows = jnp.where(live_mask[:, None], flat_rows[picked], jnp.zeros((), jnp.bfloat16))
        mixed = jnp.dot(chosen_rows, probe_proj, preferred_element_type=jnp.float32).astype(jnp.bfloat16)
        gram_full = lax.dot_general(chosen_rows, mixed, (((0,), (0,)), ((), ())), preferred_element_type=jnp.float32) / ROW_MEAN
        panel_image = jnp.dot(weight, gram_full.astype(jnp.bfloat16), preferred_element_type=jnp.float32)
        return running + panel_image, None

    basis, _ = lax.scan(expert_panel, jnp.zeros((D, P_SIZE), jnp.float32), (down_weight, starts, counts))
    basis_bf = basis.astype(jnp.bfloat16)

    def coefficient_block(weight):
        return lax.dot_general(basis_bf, weight, (((0,), (0,)), ((), ())), preferred_element_type=jnp.float32)

    coefficients = lax.map(coefficient_block, down_weight)
    return (basis, coefficients)
```

```python
import jax
import jax.numpy as jnp
from jax import lax
from jax.sharding import Mesh, PartitionSpec as P

F32 = jnp.float32
BF16 = jnp.bfloat16


def contract(a, b, ca, cb):
    return lax.dot_general(a, b, (((ca,), (cb,)), ((), ())), preferred_element_type=F32)


def swap(value, axes):
    return lax.all_to_all(value, axes, split_axis=0, concat_axis=0, tiled=False)


def body(hidden_rows, routes, down_weight, probe):
    weight = down_weight[0]
    tokens, top, width = hidden_rows.shape
    nx, ny, nc, nz = (lax.axis_size(a) for a in ("x", "y", "c", "z"))
    experts = nx * ny * nc
    chips = nx * ny
    capacity = 2 * tokens * top // experts
    row_mean = tokens * top * nz
    panel = probe.shape[1]

    expert_ids = routes.reshape(-1)
    named = (expert_ids[:, None] == jnp.arange(experts, dtype=jnp.int32)[None, :])
    onehot = named.astype(BF16)
    count = tokens * top
    earlier = jnp.tril(jnp.ones((count, count), BF16), -1)
    before = contract(earlier, onehot, 1, 0)
    position = jnp.sum(jnp.where(named, before, 0.0), axis=1).astype(jnp.int32)
    slot = expert_ids * capacity + position
    pick = (jnp.arange(experts * capacity, dtype=jnp.int32)[:, None] == slot[None, :]).astype(BF16)
    outgoing = contract(pick, hidden_rows.reshape(-1, width), 1, 0).astype(BF16)
    arrived = swap(outgoing.reshape(experts, capacity, width), ("x", "y", "c"))
    rows = arrived.reshape(-1, width)

    proj_part = contract(weight, probe, 0, 0)
    proj_own = jnp.sum(swap(proj_part.reshape(nz, width // nz, panel), "z"), axis=0).astype(BF16)
    probe_proj = lax.all_gather(proj_own, "z", axis=0, tiled=True)

    mixed = jnp.dot(rows, probe_proj, preferred_element_type=F32).astype(BF16)
    gram_part = contract(rows, mixed, 0, 0).astype(BF16)
    gram_own = jnp.sum(swap(gram_part.reshape(nz, width // nz, panel), "z").astype(F32), axis=0)
    gram = lax.all_gather((gram_own / row_mean).astype(BF16), "z", axis=0, tiled=True)

    image = jnp.dot(weight, gram, preferred_element_type=F32).astype(BF16)
    half = panel // nc
    depth = image.shape[0]
    core = lax.axis_index("c")
    kept = lax.dynamic_slice_in_dim(image, core * half, half, 1)
    given = lax.dynamic_slice_in_dim(image, (1 - core) * half, half, 1)
    flip = [(i, 1 - i) for i in range(nc)]
    chip_sum = kept.astype(F32) + lax.ppermute(given, "c", flip).astype(F32)
    pieces = swap(chip_sum.astype(BF16).reshape(chips, depth // chips, half), ("x", "y"))
    own = jnp.sum(pieces.astype(F32), axis=0)

    rows_own = depth // chips // nc
    mine = lax.dynamic_slice_in_dim(own, core * rows_own, rows_own, 0)
    other = lax.ppermute(lax.dynamic_slice_in_dim(own, (1 - core) * rows_own, rows_own, 0), "c", flip)
    basis_rows = jnp.where(core == 0, jnp.concatenate([mine, other], 1), jnp.concatenate([other, mine], 1))

    spread = swap(jnp.broadcast_to(own.astype(BF16)[None], (chips,) + own.shape), ("x", "y"))
    basis_half = spread.reshape(depth, half)
    basis = lax.all_gather(basis_half, "c", axis=1, tiled=True)
    coef_part = contract(basis, weight, 0, 0).astype(BF16)
    coef_split = coef_part.reshape(panel, nz, width // nz).transpose(1, 0, 2)
    coefficients = jnp.sum(swap(coef_split, "z").astype(F32), axis=0)
    return basis_rows, coefficients[None]


def solution(mesh):
    grid = Mesh(mesh.devices.reshape(4, 8, 2, 8), ("x", "y", "c", "z"))
    expert = ("x", "y", "c")
    in_specs = (
        P(expert + ("z",), None, None),
        P(expert + ("z",), None),
        P(expert, "z", None),
        P("z", None),
    )
    out_specs = (P(("z",) + expert, None), P(expert, None, "z"))
    return jax.shard_map(body, mesh=grid, in_specs=in_specs, out_specs=out_specs, check_vma=False)
```

```python
import functools

import jax
import jax.numpy as jnp
from jax import lax
from jax.experimental import pallas as pl
from jax.experimental.pallas import tpu as pltpu
from jax.sharding import Mesh, PartitionSpec as P

F32 = jnp.float32
BF16 = jnp.bfloat16
VMEM_BYTES = 16 * 1024 * 1024
WIDE_BYTES = 125 * 512 * 1024


def contract(a, b, ca, cb):
    return lax.dot_general(a, b, (((ca,), (cb,)), ((), ())), preferred_element_type=F32)


def swap(value, axes):
    return lax.all_to_all(value, axes, split_axis=0, concat_axis=0, tiled=False)


def share(value, axes, count):
    copies = jnp.broadcast_to(value[None], (count,) + value.shape)
    return swap(copies, axes).reshape(-1, value.shape[1])


VMEM = pl.BlockSpec(memory_space=pltpu.VMEM)
SMEM = pl.BlockSpec(memory_space=pltpu.SMEM)
HBM = pl.BlockSpec(memory_space=pltpu.MemorySpace.HBM)


def call(kernel, outs, flops, operands, in_specs=None, out_specs=None, scratch=(), limit=VMEM_BYTES):
    sizes = [a.size * a.dtype.itemsize for a in tuple(operands) + tuple(outs)]
    out = pl.pallas_call(
        kernel,
        out_shape=outs,
        in_specs=in_specs or [VMEM] * len(operands),
        out_specs=out_specs or [VMEM] * len(outs),
        scratch_shapes=scratch,
        compiler_params=pltpu.CompilerParams(vmem_limit_bytes=limit),
        cost_estimate=pl.CostEstimate(flops=flops, bytes_accessed=sum(sizes), transcendentals=0),
    )(*operands)
    return out[0] if len(outs) == 1 else out


def dispatch_kernel(capacity, routes_ref, rows_hbm, out_hbm, rows_ref, out_ref, in_sem, out_sem):
    top, tokens = routes_ref.shape
    count = tokens * top
    experts = out_ref.shape[0] // capacity
    fetch = pltpu.make_async_copy(rows_hbm, rows_ref, in_sem)
    fetch.start()

    def iota(dims, axis):
        return lax.broadcasted_iota(jnp.int32, dims, axis)

    def flag(condition):
        return jnp.where(condition, 1.0, 0.0).astype(BF16)

    spread = flag(iota((top, count), 0) == iota((top, count), 1) % top)
    token = flag(iota((tokens, count), 0) == iota((tokens, count), 1) // top)
    names = contract(routes_ref[...].astype(F32).astype(BF16), spread, 0, 0)
    expert = jnp.sum(names * token.astype(F32), axis=0, keepdims=True).astype(jnp.int32)
    named = flag(iota((experts, count), 0) == expert)
    by_token = contract(named, token, 1, 1).astype(BF16)
    earlier = flag(iota((tokens, tokens), 0) < iota((tokens, tokens), 1))
    before = jnp.dot(by_token, earlier, preferred_element_type=F32).astype(BF16)
    position = jnp.sum(jnp.dot(before, token, preferred_element_type=F32) * named.astype(F32), axis=0, keepdims=True)
    slot = expert * capacity + position.astype(jnp.int32)

    block = 256
    fetch.wait()
    rows = rows_ref[...]
    sends = []
    for i in range(out_ref.shape[0] // block):
        part = pl.ds(i * block, block)
        pick = flag(iota((block, count), 0) + i * block == slot)
        out_ref[part, :] = jnp.dot(pick, rows, preferred_element_type=F32).astype(BF16)
        sends.append(pltpu.make_async_copy(out_ref.at[part, :], out_hbm.at[part, :], out_sem.at[i]))
        sends[-1].start()
    for send in sends:
        send.wait()


def probe_kernel(quarter_ref, weight_ref, probe_ref, kept_ref, given_ref):
    quarter = quarter_ref[0]
    size = kept_ref.shape[0]
    probe = probe_ref[...]
    for step in (3, 2, 1, 0):
        start = pl.multiple_of((quarter ^ step) * size, size)
        part = contract(weight_ref[:, pl.ds(start, size)], probe, 0, 0)
        if step == 0:
            kept_ref[...] = part
        else:
            given_ref[step - 1] = part.astype(BF16)


def gram_kernel(quarter_ref, rows_ref, proj0, proj1, proj2, proj3, out_ref, proj_ref):
    quarter = quarter_ref[0]
    block = 256
    count, width = rows_ref.shape
    size = out_ref.shape[2]
    depth = proj0.shape[0]
    for step, part in enumerate((proj0, proj1, proj2, proj3)):
        proj_ref[pl.ds(pl.multiple_of((quarter ^ step) * depth, depth), depth), :] = part[...]
    proj = proj_ref[...]
    turned = []
    for i in range(count // block):
        mixed = jnp.dot(rows_ref[i * block : (i + 1) * block, :], proj, preferred_element_type=F32)
        turned.append(mixed.astype(BF16).T)
    turned = jnp.concatenate(turned, axis=1)
    for i in range(0, width, block):
        part = jnp.dot(turned, rows_ref[:, i : i + block], preferred_element_type=F32).astype(BF16)
        for j in range(0, block, size):
            out_ref[(i + j) // size] = part[:, j : j + size]


def coef_kernel(basis_ref, weight_ref, out_ref):
    block = 256
    size = out_ref.shape[2]
    turned = basis_ref[...].T
    for i in range(0, weight_ref.shape[1], block):
        part = jnp.dot(turned, weight_ref[:, i : i + block], preferred_element_type=F32).astype(BF16)
        for j in range(0, block, size):
            out_ref[(i + j) // size] = part[:, j : j + size]


def body(hidden_rows, routes, down_weight, probe):
    weight = down_weight[0]
    tokens, top, width = hidden_rows.shape
    nx, ny, nc, nz = (lax.axis_size(a) for a in ("x", "y", "c", "z"))
    experts = nx * ny * nc
    chips = nx * ny
    capacity = 2 * tokens * top // experts
    row_mean = tokens * top * nz
    depth, panel = probe.shape
    half = panel // nc
    block = width // nz
    count = tokens * top
    core = lax.axis_index("c")
    me = lax.axis_index("z")

    def across(value, axis, size, step):
        return lax.ppermute(value, axis, [(i, i ^ step) for i in range(size)])

    def shape(dims, dtype):
        return jax.ShapeDtypeStruct(dims, dtype)

    slots = experts * capacity
    outgoing = call(
        functools.partial(dispatch_kernel, capacity),
        [shape((slots, width), BF16)],
        2 * slots * count * width,
        [routes.T, hidden_rows.reshape(count, width)],
        [VMEM, HBM],
        [HBM],
        [
            pltpu.VMEM((count, width), BF16),
            pltpu.VMEM((slots, width), BF16),
            pltpu.SemaphoreType.DMA,
            pltpu.SemaphoreType.DMA((slots // 256,)),
        ],
        WIDE_BYTES,
    )
    rows = swap(outgoing.reshape(experts, capacity, width), ("x", "y", "c")).reshape(slots, width)

    quarter = (me % 4)[None]
    four = width // 4
    kept, given = call(
        probe_kernel,
        [shape((four, panel), F32), shape((3, four, panel), BF16)],
        2 * depth * width * panel,
        [quarter, weight, probe],
        [SMEM, VMEM, VMEM],
    )
    proj = kept + sum(across(given[step - 1], "z", nz, step).astype(F32) for step in (3, 2, 1))
    proj = (proj + across(proj.astype(BF16), "z", nz, 4).astype(F32)).astype(BF16)
    quarters = [across(proj, "z", nz, step) for step in (3, 2, 1)]

    gram_part = call(
        gram_kernel,
        [shape((nz, panel, block), BF16)],
        4 * slots * width * panel,
        [quarter, rows, proj] + quarters[::-1],
        [SMEM] + [VMEM] * 5,
        None,
        [pltpu.VMEM((width, panel), BF16)],
    )
    gram_own = jnp.sum(swap(gram_part, "z").astype(F32), axis=0) / row_mean
    gram = swap(jnp.broadcast_to(gram_own.astype(BF16)[None], gram_part.shape), "z")
    gram = gram.transpose(1, 0, 2).reshape(panel, width)

    image = contract(weight, gram, 1, 1).astype(BF16)
    kept = lax.dynamic_slice_in_dim(image, core * half, half, 1)
    given = lax.dynamic_slice_in_dim(image, (1 - core) * half, half, 1)
    came = lax.dynamic_index_in_dim(lax.all_gather(given, "c"), 1 - core, 0, False)
    chip_sum = kept.astype(F32) + came.astype(F32)
    pieces = swap(chip_sum.astype(BF16).reshape(chips, depth // chips, half), ("x", "y"))
    own = jnp.sum(pieces.astype(F32), axis=0).astype(BF16)
    basis_half = share(own, ("x", "y"), chips)
    basis = lax.all_gather(basis_half, "c", axis=1, tiled=True)

    rows_own = depth // experts
    place = (lax.axis_index("x") * ny + lax.axis_index("y")) * nc + core
    basis_rows = lax.dynamic_slice_in_dim(basis, place * rows_own, rows_own, 0).astype(F32)
    coef_part = call(coef_kernel, [shape((nz, panel, block), BF16)], 2 * depth * width * panel, [basis, weight])
    coefficients = jnp.sum(swap(coef_part, "z").astype(F32), axis=0)
    return basis_rows, coefficients[None]


def solution(mesh):
    grid = Mesh(mesh.devices.reshape(4, 8, 2, 8), ("x", "y", "c", "z"))
    expert = ("x", "y", "c")
    in_specs = (
        P(expert + ("z",), None, None),
        P(expert + ("z",), None),
        P(expert, "z", None),
        P("z", None),
    )
    out_specs = (P(("z",) + expert, None), P(expert, None, "z"))
    return jax.shard_map(body, mesh=grid, in_specs=in_specs, out_specs=out_specs, check_vma=False)
```

```python
import functools

import jax
import jax.numpy as jnp
from jax import lax
from jax.experimental import pallas as pl
from jax.experimental.pallas import tpu as pltpu
from jax.sharding import Mesh, PartitionSpec as P

F32 = jnp.float32
BF16 = jnp.bfloat16
VMEM_BYTES = 16 * 1024 * 1024
WIDE_BYTES = 125 * 512 * 1024


def contract(a, b, ca, cb):
    return lax.dot_general(a, b, (((ca,), (cb,)), ((), ())), preferred_element_type=F32)


def swap(value, axes):
    return lax.all_to_all(value, axes, split_axis=0, concat_axis=0, tiled=False)


def share(value, axes, count):
    copies = jnp.broadcast_to(value[None], (count,) + value.shape)
    return swap(copies, axes).reshape(-1, value.shape[1])


VMEM = pl.BlockSpec(memory_space=pltpu.VMEM)
SMEM = pl.BlockSpec(memory_space=pltpu.SMEM)
HBM = pl.BlockSpec(memory_space=pltpu.MemorySpace.HBM)


def call(kernel, outs, flops, operands, in_specs=None, out_specs=None, scratch=(), limit=VMEM_BYTES):
    sizes = [a.size * a.dtype.itemsize for a in tuple(operands) + tuple(outs)]
    out = pl.pallas_call(
        kernel,
        out_shape=outs,
        in_specs=in_specs or [VMEM] * len(operands),
        out_specs=out_specs or [VMEM] * len(outs),
        scratch_shapes=scratch,
        compiler_params=pltpu.CompilerParams(vmem_limit_bytes=limit),
        cost_estimate=pl.CostEstimate(flops=flops, bytes_accessed=sum(sizes), transcendentals=0),
    )(*operands)
    return out[0] if len(outs) == 1 else out


def dispatch_kernel(capacity, routes_hbm, rows_hbm, out_hbm, routes_ref, rows_ref, out_ref, in_sem, out_sem):
    top, tokens = routes_ref.shape
    count = tokens * top
    experts = out_ref.shape[0] // capacity
    names = pltpu.make_async_copy(routes_hbm, routes_ref, in_sem.at[0])
    names.start()
    fetch = pltpu.make_async_copy(rows_hbm, rows_ref, in_sem.at[1])
    fetch.start()

    def iota(dims, axis):
        return lax.broadcasted_iota(jnp.int32, dims, axis)

    def flag(condition):
        return jnp.where(condition, 1.0, 0.0).astype(BF16)

    spread = flag(iota((top, count), 0) == iota((top, count), 1) % top)
    token = flag(iota((tokens, count), 0) == iota((tokens, count), 1) // top)
    earlier = flag(iota((tokens, tokens), 0) < iota((tokens, tokens), 1))
    names.wait()
    spelled = contract(routes_ref[...].astype(F32).astype(BF16), spread, 0, 0)
    expert = jnp.sum(spelled * token.astype(F32), axis=0, keepdims=True).astype(jnp.int32)
    named = flag(iota((experts, count), 0) == expert)
    by_token = contract(named, token, 1, 1).astype(BF16)
    before = jnp.dot(by_token, earlier, preferred_element_type=F32).astype(BF16)
    position = jnp.sum(jnp.dot(before, token, preferred_element_type=F32) * named.astype(F32), axis=0, keepdims=True)
    slot = expert * capacity + position.astype(jnp.int32)

    block = 256
    fetch.wait()
    rows = rows_ref[...]
    sends = []
    for i in range(out_ref.shape[0] // block):
        part = pl.ds(i * block, block)
        pick = flag(iota((block, count), 0) + i * block == slot)
        out_ref[part, :] = jnp.dot(pick, rows, preferred_element_type=F32).astype(BF16)
        sends.append(pltpu.make_async_copy(out_ref.at[part, :], out_hbm.at[part, :], out_sem.at[i]))
        sends[-1].start()
    for send in sends:
        send.wait()


def probe_kernel(quarter_ref, weight_ref, probe_ref, kept_ref, given_ref):
    quarter = quarter_ref[0]
    size = kept_ref.shape[0]
    probe = probe_ref[...]
    for step in (3, 2, 1, 0):
        start = pl.multiple_of((quarter ^ step) * size, size)
        part = contract(weight_ref[:, pl.ds(start, size)], probe, 0, 0)
        if step == 0:
            kept_ref[...] = part
        else:
            given_ref[step - 1] = part.astype(BF16)


def gram_kernel(quarter_ref, rows_ref, proj0, proj1, proj2, proj3, out_ref, proj_ref):
    quarter = quarter_ref[0]
    block = 256
    count, width = rows_ref.shape
    size = out_ref.shape[2]
    depth = proj0.shape[0]
    for step, part in enumerate((proj0, proj1, proj2, proj3)):
        proj_ref[pl.ds(pl.multiple_of((quarter ^ step) * depth, depth), depth), :] = part[...]
    proj = proj_ref[...]
    turned = []
    for i in range(count // block):
        mixed = jnp.dot(rows_ref[i * block : (i + 1) * block, :], proj, preferred_element_type=F32)
        turned.append(mixed.astype(BF16).T)
    turned = jnp.concatenate(turned, axis=1)
    for i in range(0, width, block):
        part = jnp.dot(turned, rows_ref[:, i : i + block], preferred_element_type=F32).astype(BF16)
        for j in range(0, block, size):
            out_ref[(i + j) // size] = part[:, j : j + size]


def share_kernel(scale, parts_ref, out_ref):
    total = jnp.sum(parts_ref[...].astype(F32), axis=0) * scale
    value = total.astype(BF16).T
    for i in range(out_ref.shape[0]):
        out_ref[i] = value


def image_kernel(core_ref, weight_ref, gram_ref, kept_ref, given_ref):
    half = kept_ref.shape[1]
    image = jnp.dot(weight_ref[...], gram_ref[...], preferred_element_type=F32)
    left, right = image[:, :half], image[:, half:]
    first = core_ref[0] == 0
    kept_ref[...] = jnp.where(first, left, right)
    given_ref[...] = jnp.where(first, right, left).astype(BF16)


def coef_kernel(weight_ref, basis_ref, out_ref):
    size = out_ref.shape[1]
    basis = basis_ref[...]
    for i in range(0, weight_ref.shape[1], 2 * size):
        part = contract(weight_ref[:, i : i + 2 * size], basis, 0, 0).astype(BF16)
        out_ref[i // size] = part[:size]
        out_ref[i // size + 1] = part[size:]


def total_kernel(parts_ref, out_ref):
    out_ref[...] = jnp.sum(parts_ref[...].astype(F32), axis=0).T


def body(hidden_rows, routes, down_weight, probe):
    weight = down_weight[0]
    tokens, top, width = hidden_rows.shape
    nx, ny, nc, nz = (lax.axis_size(a) for a in ("x", "y", "c", "z"))
    experts = nx * ny * nc
    chips = nx * ny
    capacity = 2 * tokens * top // experts
    row_mean = tokens * top * nz
    depth, panel = probe.shape
    half = panel // nc
    block = width // nz
    count = tokens * top
    core = lax.axis_index("c")
    me = lax.axis_index("z")

    def across(value, axis, size, step):
        return lax.ppermute(value, axis, [(i, i ^ step) for i in range(size)])

    def shape(dims, dtype):
        return jax.ShapeDtypeStruct(dims, dtype)

    slots = experts * capacity
    outgoing = call(
        functools.partial(dispatch_kernel, capacity),
        [shape((slots, width), BF16)],
        2 * slots * count * width,
        [routes.T, hidden_rows.reshape(count, width)],
        [HBM, HBM],
        [HBM],
        [
            pltpu.VMEM((top, tokens), jnp.int32),
            pltpu.VMEM((count, width), BF16),
            pltpu.VMEM((slots, width), BF16),
            pltpu.SemaphoreType.DMA((2,)),
            pltpu.SemaphoreType.DMA((slots // 256,)),
        ],
        WIDE_BYTES,
    )
    rows = swap(outgoing.reshape(experts, capacity, width), ("x", "y", "c")).reshape(slots, width)

    quarter = (me % 4)[None]
    four = width // 4
    kept, given = call(
        probe_kernel,
        [shape((four, panel), F32), shape((3, four, panel), BF16)],
        2 * depth * width * panel,
        [quarter, weight, probe],
        [SMEM, VMEM, VMEM],
    )
    proj = kept + sum(across(given[step - 1], "z", nz, step).astype(F32) for step in (3, 2, 1))
    proj = (proj + across(proj.astype(BF16), "z", nz, 4).astype(F32)).astype(BF16)
    quarters = [across(proj, "z", nz, step) for step in (3, 2, 1)]

    gram_part = call(
        gram_kernel,
        [shape((nz, panel, block), BF16)],
        4 * slots * width * panel,
        [quarter, rows, proj] + quarters[::-1],
        [SMEM] + [VMEM] * 5,
        None,
        [pltpu.VMEM((width, panel), BF16)],
    )
    copies = call(
        functools.partial(share_kernel, 1.0 / row_mean),
        [shape((nz, block, panel), BF16)],
        nz * block * panel,
        [swap(gram_part, "z")],
    )
    gram = swap(copies, "z").reshape(width, panel)

    kept, given = call(
        image_kernel,
        [shape((depth, half), F32), shape((depth, half), BF16)],
        2 * depth * width * panel,
        [core[None], weight, gram],
        [SMEM, VMEM, VMEM],
    )
    chip_sum = kept + lax.dynamic_index_in_dim(lax.all_gather(given, "c"), 1 - core, 0, False).astype(F32)
    pieces = swap(chip_sum.astype(BF16).reshape(chips, depth // chips, half), ("x", "y"))
    own = jnp.sum(pieces.astype(F32), axis=0).astype(BF16)
    basis_half = share(own, ("x", "y"), chips)
    basis = lax.all_gather(basis_half, "c", axis=1, tiled=True)

    rows_own = depth // experts
    place = (lax.axis_index("x") * ny + lax.axis_index("y")) * nc + core
    basis_rows = lax.dynamic_slice_in_dim(basis, place * rows_own, rows_own, 0).astype(F32)
    coef_part = call(coef_kernel, [shape((nz, block, panel), BF16)], 2 * depth * width * panel, [weight, basis])
    coefficients = call(total_kernel, [shape((panel, block), F32)], nz * block * panel, [swap(coef_part, "z")])
    return basis_rows, coefficients[None]


def solution(mesh):
    grid = Mesh(mesh.devices.reshape(4, 8, 2, 8), ("x", "y", "c", "z"))
    expert = ("x", "y", "c")
    in_specs = (
        P(expert + ("z",), None, None),
        P(expert + ("z",), None),
        P(expert, "z", None),
        P("z", None),
    )
    out_specs = (P(("z",) + expert, None), P(expert, None, "z"))
    return jax.shard_map(body, mesh=grid, in_specs=in_specs, out_specs=out_specs, check_vma=False)
```

```python
import functools

import jax
import jax.numpy as jnp
from jax import lax
from jax.experimental import pallas as pl
from jax.experimental.pallas import tpu as pltpu
from jax.sharding import Mesh, PartitionSpec as P

F32 = jnp.float32
BF16 = jnp.bfloat16
VMEM_BYTES = 16 * 1024 * 1024
WIDE_BYTES = 125 * 512 * 1024


def contract(a, b, ca, cb):
    return lax.dot_general(a, b, (((ca,), (cb,)), ((), ())), preferred_element_type=F32)


def swap(value, axes):
    return lax.all_to_all(value, axes, split_axis=0, concat_axis=0, tiled=False)


def share(value, axes, count):
    copies = jnp.broadcast_to(value[None], (count,) + value.shape)
    return swap(copies, axes).reshape(-1, value.shape[1])


VMEM = pl.BlockSpec(memory_space=pltpu.VMEM)
SMEM = pl.BlockSpec(memory_space=pltpu.SMEM)
HBM = pl.BlockSpec(memory_space=pltpu.MemorySpace.HBM)


def call(kernel, outs, flops, operands, in_specs=None, out_specs=None, scratch=(), limit=VMEM_BYTES):
    sizes = [a.size * a.dtype.itemsize for a in tuple(operands) + tuple(outs)]
    out = pl.pallas_call(
        kernel,
        out_shape=outs,
        in_specs=in_specs or [VMEM] * len(operands),
        out_specs=out_specs or [VMEM] * len(outs),
        scratch_shapes=scratch,
        compiler_params=pltpu.CompilerParams(vmem_limit_bytes=limit),
        cost_estimate=pl.CostEstimate(flops=flops, bytes_accessed=sum(sizes), transcendentals=0),
    )(*operands)
    return out[0] if len(outs) == 1 else out


def dispatch_kernel(capacity, routes_hbm, rows_hbm, out_hbm, routes_ref, rows_ref, out_ref, in_sem, out_sem):
    top, tokens = routes_ref.shape
    count = tokens * top
    experts = out_ref.shape[0] // capacity
    names = pltpu.make_async_copy(routes_hbm, routes_ref, in_sem.at[0])
    names.start()
    fetch = pltpu.make_async_copy(rows_hbm, rows_ref, in_sem.at[1])
    fetch.start()

    def iota(dims, axis):
        return lax.broadcasted_iota(jnp.int32, dims, axis)

    def flag(condition):
        return jnp.where(condition, 1.0, 0.0).astype(BF16)

    spread = flag(iota((top, count), 0) == iota((top, count), 1) % top)
    token = flag(iota((tokens, count), 0) == iota((tokens, count), 1) // top)
    earlier = flag(iota((tokens, tokens), 0) < iota((tokens, tokens), 1))
    names.wait()
    spelled = contract(routes_ref[...].astype(F32).astype(BF16), spread, 0, 0)
    expert = jnp.sum(spelled * token.astype(F32), axis=0, keepdims=True).astype(jnp.int32)
    named = flag(iota((experts, count), 0) == expert)
    by_token = contract(named, token, 1, 1).astype(BF16)
    before = jnp.dot(by_token, earlier, preferred_element_type=F32).astype(BF16)
    position = jnp.sum(jnp.dot(before, token, preferred_element_type=F32) * named.astype(F32), axis=0, keepdims=True)
    slot = expert * capacity + position.astype(jnp.int32)

    block = 256
    fetch.wait()
    rows = rows_ref[...]
    sends = []
    for i in range(out_ref.shape[0] // block):
        part = pl.ds(i * block, block)
        pick = flag(iota((block, count), 0) + i * block == slot)
        out_ref[part, :] = jnp.dot(pick, rows, preferred_element_type=F32).astype(BF16)
        sends.append(pltpu.make_async_copy(out_ref.at[part, :], out_hbm.at[part, :], out_sem.at[i]))
        sends[-1].start()
    for send in sends:
        send.wait()


def probe_kernel(quarter_ref, weight_ref, probe_ref, kept_ref, given_ref):
    quarter = quarter_ref[0]
    size = kept_ref.shape[0]
    probe = probe_ref[...]
    for step in (3, 2, 1, 0):
        start = pl.multiple_of((quarter ^ step) * size, size)
        part = contract(weight_ref[:, pl.ds(start, size)], probe, 0, 0)
        if step == 0:
            kept_ref[...] = part
        else:
            given_ref[step - 1] = part.astype(BF16)


def gram_kernel(quarter_ref, rows_ref, proj0, proj1, proj2, proj3, out_ref, proj_ref):
    quarter = quarter_ref[0]
    block = 256
    count, width = rows_ref.shape
    size = out_ref.shape[2]
    depth = proj0.shape[0]
    for step, part in enumerate((proj0, proj1, proj2, proj3)):
        proj_ref[pl.ds(pl.multiple_of((quarter ^ step) * depth, depth), depth), :] = part[...]
    proj = proj_ref[...]
    turned = []
    for i in range(count // block):
        mixed = jnp.dot(rows_ref[i * block : (i + 1) * block, :], proj, preferred_element_type=F32)
        turned.append(mixed.astype(BF16).T)
    turned = jnp.concatenate(turned, axis=1)
    for i in range(0, width, block):
        part = jnp.dot(turned, rows_ref[:, i : i + block], preferred_element_type=F32).astype(BF16)
        for j in range(0, block, size):
            out_ref[(i + j) // size] = part[:, j : j + size]


def share_kernel(scale, parts_ref, out_ref):
    cores, devices, _, half = out_ref.shape
    total = jnp.sum(parts_ref[...].astype(F32), axis=0) * scale
    value = total.astype(BF16).T
    for core in range(cores):
        for device in range(devices):
            out_ref[core, device] = value[:, core * half : (core + 1) * half]


def image_kernel(core_ref, own_ref, other_hbm, gram_ref, out_ref, other_ref, sems):
    core = core_ref[0]
    block = own_ref.shape[0] // sems.shape[0]
    parts = [pl.ds(i * block, block) for i in range(sems.shape[0])]
    fetches = [
        pltpu.make_async_copy(other_hbm.at[part, :], other_ref.at[part, :], sems.at[i]) for i, part in enumerate(parts)
    ]
    for fetch in fetches:
        fetch.start()
    own, other = gram_ref[core], gram_ref[1 - core]
    for part, fetch in zip(parts, fetches):
        image = jnp.dot(own_ref[part, :], own, preferred_element_type=F32)
        fetch.wait()
        image += jnp.dot(other_ref[part, :], other, preferred_element_type=F32)
        out_ref[part, :] = image.astype(BF16)


def coef_kernel(core_ref, own_ref, other_hbm, basis_ref, out_hbm, other_ref, out_ref, in_sems, out_sems):
    core = core_ref[0]
    size = out_ref.shape[3]
    block = own_ref.shape[1] // in_sems.shape[0]
    parts = [pl.ds(i * block, block) for i in range(in_sems.shape[0])]
    fetches = [
        pltpu.make_async_copy(other_hbm.at[:, part], other_ref.at[:, part], in_sems.at[i])
        for i, part in enumerate(parts)
    ]
    for fetch in fetches:
        fetch.start()
    turned = basis_ref[...].T
    sends = []
    for turn, (which, weight_ref) in enumerate(((core, own_ref), (1 - core, other_ref))):
        for i, part in enumerate(parts):
            if turn == 1:
                fetches[i].wait()
            value = jnp.dot(turned, weight_ref[:, part], preferred_element_type=F32).astype(BF16)
            for j in range(block // size):
                out_ref[turn, i * (block // size) + j] = value[:, j * size : (j + 1) * size]
        sends.append(pltpu.make_async_copy(out_ref.at[turn], out_hbm.at[which], out_sems.at[turn]))
        sends[-1].start()
    for send in sends:
        send.wait()


def total_kernel(parts_ref, out_ref):
    size = parts_ref.shape[2]
    for core in range(parts_ref.shape[0]):
        out_ref[core * size : (core + 1) * size, :] = jnp.sum(parts_ref[core].astype(F32), axis=0)


def body(hidden_rows, routes, down_weight, probe):
    weight = down_weight[0]
    tokens, top, width = hidden_rows.shape
    nx, ny, nc, nz = (lax.axis_size(a) for a in ("x", "y", "c", "z"))
    experts = nx * ny * nc
    chips = nx * ny
    capacity = 2 * tokens * top // experts
    row_mean = tokens * top * nz
    depth, panel = probe.shape
    half = panel // nc
    block = width // nz
    count = tokens * top
    core = lax.axis_index("c")
    me = lax.axis_index("z")

    def across(value, axis, size, step):
        return lax.ppermute(value, axis, [(i, i ^ step) for i in range(size)])

    def shape(dims, dtype):
        return jax.ShapeDtypeStruct(dims, dtype)

    slots = experts * capacity
    outgoing = call(
        functools.partial(dispatch_kernel, capacity),
        [shape((slots, width), BF16)],
        2 * slots * count * width,
        [routes.T, hidden_rows.reshape(count, width)],
        [HBM, HBM],
        [HBM],
        [
            pltpu.VMEM((top, tokens), jnp.int32),
            pltpu.VMEM((count, width), BF16),
            pltpu.VMEM((slots, width), BF16),
            pltpu.SemaphoreType.DMA((2,)),
            pltpu.SemaphoreType.DMA((slots // 256,)),
        ],
        WIDE_BYTES,
    )
    rows = swap(outgoing.reshape(experts, capacity, width), ("x", "y", "c")).reshape(slots, width)

    quarter = (me % 4)[None]
    four = width // 4
    kept, given = call(
        probe_kernel,
        [shape((four, panel), F32), shape((3, four, panel), BF16)],
        2 * depth * width * panel,
        [quarter, weight, probe],
        [SMEM, VMEM, VMEM],
    )
    proj = kept + sum(across(given[step - 1], "z", nz, step).astype(F32) for step in (3, 2, 1))
    proj = (proj + across(proj.astype(BF16), "z", nz, 4).astype(F32)).astype(BF16)
    quarters = [across(proj, "z", nz, step) for step in (3, 2, 1)]
    neighbour = across(weight, "c", nc, 1)

    gram_part = call(
        gram_kernel,
        [shape((nz, panel, block), BF16)],
        4 * slots * width * panel,
        [quarter, rows, proj] + quarters[::-1],
        [SMEM] + [VMEM] * 5,
        None,
        [pltpu.VMEM((width, panel), BF16)],
    )
    copies = call(
        functools.partial(share_kernel, 1.0 / row_mean),
        [shape((nc, nz, block, half), BF16)],
        nz * block * panel,
        [swap(gram_part, "z")],
    )
    gram = swap(copies.reshape(nc * nz, block, half), ("c", "z")).reshape(nc, width, half)

    image = call(
        image_kernel,
        [shape((depth, half), BF16)],
        2 * depth * width * panel,
        [core[None], weight, neighbour, gram],
        [SMEM, VMEM, HBM, VMEM],
        None,
        [pltpu.VMEM((depth, width), BF16), pltpu.SemaphoreType.DMA((4,))],
    )
    pieces = swap(image.reshape(chips, depth // chips, half), ("x", "y"))
    own = jnp.sum(pieces.astype(F32), axis=0)
    basis = share(own.astype(BF16), ("x", "y"), chips)

    rows_own = depth // experts
    mine = lax.dynamic_slice_in_dim(own, core * rows_own, rows_own, 0)
    other = across(lax.dynamic_slice_in_dim(own, (1 - core) * rows_own, rows_own, 0), "c", nc, 1)
    basis_rows = jnp.where(core == 0, jnp.concatenate([mine, other], 1), jnp.concatenate([other, mine], 1))

    coef_part = call(
        coef_kernel,
        [shape((nc, nz, half, block), BF16)],
        2 * depth * width * panel,
        [core[None], weight, neighbour, basis],
        [SMEM, VMEM, HBM, VMEM],
        [HBM],
        [
            pltpu.VMEM((depth, width), BF16),
            pltpu.VMEM((nc, nz, half, block), BF16),
            pltpu.SemaphoreType.DMA((4,)),
            pltpu.SemaphoreType.DMA((nc,)),
        ],
    )
    arrived = swap(coef_part.reshape(nc * nz, half, block), ("c", "z")).reshape(nc, nz, half, block)
    coefficients = call(total_kernel, [shape((panel, block), F32)], nz * block * panel, [arrived])
    return basis_rows, coefficients[None]


def solution(mesh):
    grid = Mesh(mesh.devices.reshape(4, 8, 2, 8), ("x", "y", "c", "z"))
    expert = ("x", "y", "c")
    in_specs = (
        P(expert + ("z",), None, None),
        P(expert + ("z",), None),
        P(expert, "z", None),
        P("z", None),
    )
    out_specs = (P(("z",) + expert, None), P(expert, None, "z"))
    return jax.shard_map(body, mesh=grid, in_specs=in_specs, out_specs=out_specs, check_vma=False)
```

```python
import functools

import jax
import jax.numpy as jnp
from jax import lax
from jax.experimental import pallas as pl
from jax.experimental.pallas import tpu as pltpu
from jax.sharding import Mesh, PartitionSpec as P

F32 = jnp.float32
BF16 = jnp.bfloat16
VMEM_BYTES = 16 * 1024 * 1024
WIDE_BYTES = 125 * 512 * 1024


def contract(a, b, ca, cb):
    return lax.dot_general(a, b, (((ca,), (cb,)), ((), ())), preferred_element_type=F32)


def swap(value, axes):
    return lax.all_to_all(value, axes, split_axis=0, concat_axis=0, tiled=False)


def share(value, axes, count):
    copies = jnp.broadcast_to(value[None], (count,) + value.shape)
    return swap(copies, axes).reshape(-1, value.shape[1])


VMEM = pl.BlockSpec(memory_space=pltpu.VMEM)
SMEM = pl.BlockSpec(memory_space=pltpu.SMEM)
HBM = pl.BlockSpec(memory_space=pltpu.MemorySpace.HBM)


def call(kernel, outs, flops, operands, in_specs=None, out_specs=None, scratch=(), limit=VMEM_BYTES):
    sizes = [a.size * a.dtype.itemsize for a in tuple(operands) + tuple(outs)]
    out = pl.pallas_call(
        kernel,
        out_shape=outs,
        in_specs=in_specs or [VMEM] * len(operands),
        out_specs=out_specs or [VMEM] * len(outs),
        scratch_shapes=scratch,
        compiler_params=pltpu.CompilerParams(vmem_limit_bytes=limit),
        cost_estimate=pl.CostEstimate(flops=flops, bytes_accessed=sum(sizes), transcendentals=0),
    )(*operands)
    return out[0] if len(outs) == 1 else out


def dispatch_kernel(capacity, routes_hbm, rows_hbm, out_hbm, routes_ref, rows_ref, out_ref, in_sem, out_sem):
    top, tokens = routes_ref.shape
    count = tokens * top
    experts = out_ref.shape[0] // capacity
    names = pltpu.make_async_copy(routes_hbm, routes_ref, in_sem.at[0])
    names.start()
    fetch = pltpu.make_async_copy(rows_hbm, rows_ref, in_sem.at[1])
    fetch.start()

    def iota(dims, axis):
        return lax.broadcasted_iota(jnp.int32, dims, axis)

    def flag(condition):
        return jnp.where(condition, 1.0, 0.0).astype(BF16)

    spread = flag(iota((top, count), 0) == iota((top, count), 1) % top)
    token = flag(iota((tokens, count), 0) == iota((tokens, count), 1) // top)
    earlier = flag(iota((tokens, tokens), 0) < iota((tokens, tokens), 1))
    names.wait()
    spelled = contract(routes_ref[...].astype(F32).astype(BF16), spread, 0, 0)
    expert = jnp.sum(spelled * token.astype(F32), axis=0, keepdims=True).astype(jnp.int32)
    named = flag(iota((experts, count), 0) == expert)
    by_token = contract(named, token, 1, 1).astype(BF16)
    before = jnp.dot(by_token, earlier, preferred_element_type=F32).astype(BF16)
    position = jnp.sum(jnp.dot(before, token, preferred_element_type=F32) * named.astype(F32), axis=0, keepdims=True)
    slot = expert * capacity + position.astype(jnp.int32)

    block = 256
    fetch.wait()
    rows = rows_ref[...]
    sends = []
    for i in range(out_ref.shape[0] // block):
        part = pl.ds(i * block, block)
        pick = flag(iota((block, count), 0) + i * block == slot)
        out_ref[part, :] = jnp.dot(pick, rows, preferred_element_type=F32).astype(BF16)
        sends.append(pltpu.make_async_copy(out_ref.at[part, :], out_hbm.at[part, :], out_sem.at[i]))
        sends[-1].start()
    for send in sends:
        send.wait()


def probe_kernel(quarter_ref, weight_ref, probe_ref, kept_ref, given_ref):
    quarter = quarter_ref[0]
    size = kept_ref.shape[0]
    probe = probe_ref[...]
    for step in (3, 2, 1, 0):
        start = pl.multiple_of((quarter ^ step) * size, size)
        part = contract(weight_ref[:, pl.ds(start, size)], probe, 0, 0)
        if step == 0:
            kept_ref[...] = part
        else:
            given_ref[step - 1] = part.astype(BF16)


def gram_kernel(quarter_ref, rows_ref, proj3, proj2, proj1, proj0, out_ref, proj_ref):
    quarter = quarter_ref[0]
    block = 256
    count, width = rows_ref.shape
    size = out_ref.shape[2]
    depth = proj0.shape[0]
    for step, part in enumerate((proj0, proj1, proj2, proj3)):
        proj_ref[pl.ds(pl.multiple_of((quarter ^ step) * depth, depth), depth), :] = part[...]
    proj = proj_ref[...]
    turned = []
    for i in range(count // block):
        mixed = jnp.dot(rows_ref[i * block : (i + 1) * block, :], proj, preferred_element_type=F32)
        turned.append(mixed.astype(BF16).T)
    turned = jnp.concatenate(turned, axis=1)
    for i in range(0, width, block):
        part = jnp.dot(turned, rows_ref[:, i : i + block], preferred_element_type=F32).astype(BF16)
        for j in range(0, block, size):
            out_ref[(i + j) // size] = part[:, j : j + size]


def share_kernel(scale, parts_ref, out_ref):
    cores, devices, _, half = out_ref.shape
    total = jnp.sum(parts_ref[...].astype(F32), axis=0) * scale
    value = total.astype(BF16).T
    for core in range(cores):
        for device in range(devices):
            out_ref[core, device] = value[:, core * half : (core + 1) * half]


def image_kernel(core_ref, own_ref, other_hbm, gram_ref, out_ref, other_ref, sems):
    core = core_ref[0]
    block = own_ref.shape[0] // sems.shape[0]
    parts = [pl.ds(i * block, block) for i in range(sems.shape[0])]
    fetches = [
        pltpu.make_async_copy(other_hbm.at[part, :], other_ref.at[part, :], sems.at[i]) for i, part in enumerate(parts)
    ]
    for fetch in fetches:
        fetch.start()
    own, other = gram_ref[core], gram_ref[1 - core]
    for part, fetch in zip(parts, fetches):
        image = jnp.dot(own_ref[part, :], own, preferred_element_type=F32)
        fetch.wait()
        image += jnp.dot(other_ref[part, :], other, preferred_element_type=F32)
        out_ref[part, :] = image.astype(BF16)


def coef_kernel(core_ref, own_ref, other_hbm, basis_ref, out_hbm, other_ref, out_ref, in_sems, out_sems):
    core = core_ref[0]
    size = out_ref.shape[3]
    block = own_ref.shape[1] // in_sems.shape[0]
    parts = [pl.ds(i * block, block) for i in range(in_sems.shape[0])]
    fetches = [
        pltpu.make_async_copy(other_hbm.at[:, part], other_ref.at[:, part], in_sems.at[i])
        for i, part in enumerate(parts)
    ]
    for fetch in fetches:
        fetch.start()
    turned = basis_ref[...].T
    sends = []
    for turn, (which, weight_ref) in enumerate(((core, own_ref), (1 - core, other_ref))):
        for i, part in enumerate(parts):
            if turn == 1:
                fetches[i].wait()
            value = jnp.dot(turned, weight_ref[:, part], preferred_element_type=F32).astype(BF16)
            for j in range(block // size):
                out_ref[turn, i * (block // size) + j] = value[:, j * size : (j + 1) * size]
        sends.append(pltpu.make_async_copy(out_ref.at[turn], out_hbm.at[which], out_sems.at[turn]))
        sends[-1].start()
    for send in sends:
        send.wait()


def total_kernel(parts_ref, out_ref):
    size = parts_ref.shape[2]
    for core in range(parts_ref.shape[0]):
        out_ref[core * size : (core + 1) * size, :] = jnp.sum(parts_ref[core].astype(F32), axis=0)


def body(hidden_rows, routes, down_weight, probe):
    weight = down_weight[0]
    tokens, top, width = hidden_rows.shape
    nx, ny, nc, nz = (lax.axis_size(a) for a in ("x", "y", "c", "z"))
    experts = nx * ny * nc
    chips = nx * ny
    capacity = 2 * tokens * top // experts
    row_mean = tokens * top * nz
    depth, panel = probe.shape
    half = panel // nc
    block = width // nz
    count = tokens * top
    core = lax.axis_index("c")
    me = lax.axis_index("z")

    def across(value, axis, size, step):
        return lax.ppermute(value, axis, [(i, i ^ step) for i in range(size)])

    def shape(dims, dtype):
        return jax.ShapeDtypeStruct(dims, dtype)

    slots = experts * capacity
    outgoing = call(
        functools.partial(dispatch_kernel, capacity),
        [shape((slots, width), BF16)],
        2 * slots * count * width,
        [routes.T, hidden_rows.reshape(count, width)],
        [HBM, HBM],
        [HBM],
        [
            pltpu.VMEM((top, tokens), jnp.int32),
            pltpu.VMEM((count, width), BF16),
            pltpu.VMEM((slots, width), BF16),
            pltpu.SemaphoreType.DMA((2,)),
            pltpu.SemaphoreType.DMA((slots // 256,)),
        ],
        WIDE_BYTES,
    )
    rows = swap(outgoing.reshape(experts, capacity, width), ("x", "y", "c")).reshape(slots, width)

    quarter = (me % 4)[None]
    four = width // 4
    kept, given = call(
        probe_kernel,
        [shape((four, panel), F32), shape((3, four, panel), BF16)],
        2 * depth * width * panel,
        [quarter, weight, probe],
        [SMEM, VMEM, VMEM],
    )
    proj = kept + sum(across(given[step - 1], "z", nz, step).astype(F32) for step in (1, 2, 3))
    proj = (proj + across(proj.astype(BF16), "z", nz, 4).astype(F32)).astype(BF16)
    quarters = [across(proj, "z", nz, step) for step in (1, 2, 3)]
    neighbour = across(weight, "c", nc, 1)

    rows, neighbour = lax.optimization_barrier((rows, neighbour))

    gram_part = call(
        gram_kernel,
        [shape((nz, panel, block), BF16)],
        4 * slots * width * panel,
        [quarter, rows] + quarters[::-1] + [proj],
        [SMEM] + [VMEM] * 5,
        None,
        [pltpu.VMEM((width, panel), BF16)],
    )
    copies = call(
        functools.partial(share_kernel, 1.0 / row_mean),
        [shape((nc, nz, block, half), BF16)],
        nz * block * panel,
        [swap(gram_part, "z")],
    )
    gram = swap(copies.reshape(nc * nz, block, half), ("c", "z")).reshape(nc, width, half)

    image = call(
        image_kernel,
        [shape((depth, half), BF16)],
        2 * depth * width * panel,
        [core[None], weight, neighbour, gram],
        [SMEM, VMEM, HBM, VMEM],
        None,
        [pltpu.VMEM((depth, width), BF16), pltpu.SemaphoreType.DMA((4,))],
    )
    pieces = swap(image.reshape(chips, depth // chips, half), ("x", "y"))
    own = jnp.sum(pieces.astype(F32), axis=0)
    basis = share(own.astype(BF16), ("x", "y"), chips)

    rows_own = depth // experts
    mine = lax.dynamic_slice_in_dim(own, core * rows_own, rows_own, 0)
    other = across(lax.dynamic_slice_in_dim(own, (1 - core) * rows_own, rows_own, 0), "c", nc, 1)
    basis_rows = jnp.where(core == 0, jnp.concatenate([mine, other], 1), jnp.concatenate([other, mine], 1))

    coef_part = call(
        coef_kernel,
        [shape((nc, nz, half, block), BF16)],
        2 * depth * width * panel,
        [core[None], weight, neighbour, basis],
        [SMEM, VMEM, HBM, VMEM],
        [HBM],
        [
            pltpu.VMEM((depth, width), BF16),
            pltpu.VMEM((nc, nz, half, block), BF16),
            pltpu.SemaphoreType.DMA((4,)),
            pltpu.SemaphoreType.DMA((nc,)),
        ],
    )
    arrived = swap(coef_part.reshape(nc * nz, half, block), ("c", "z")).reshape(nc, nz, half, block)
    coefficients = call(total_kernel, [shape((panel, block), F32)], nz * block * panel, [arrived])
    return basis_rows, coefficients[None]


def solution(mesh):
    grid = Mesh(mesh.devices.reshape(4, 8, 2, 8), ("x", "y", "c", "z"))
    expert = ("x", "y", "c")
    in_specs = (
        P(expert + ("z",), None, None),
        P(expert + ("z",), None),
        P(expert, "z", None),
        P("z", None),
    )
    out_specs = (P(("z",) + expert, None), P(expert, None, "z"))
    return jax.shard_map(body, mesh=grid, in_specs=in_specs, out_specs=out_specs, check_vma=False)
```

```python
import functools

import jax
import jax.numpy as jnp
from jax import lax
from jax.experimental import pallas as pl
from jax.experimental.pallas import tpu as pltpu
from jax.sharding import Mesh, PartitionSpec as P

F32 = jnp.float32
BF16 = jnp.bfloat16
VMEM_BYTES = 16 * 1024 * 1024
WIDE_BYTES = 125 * 512 * 1024


def contract(a, b, ca, cb):
    return lax.dot_general(a, b, (((ca,), (cb,)), ((), ())), preferred_element_type=F32)


def swap(value, axes):
    return lax.all_to_all(value, axes, split_axis=0, concat_axis=0, tiled=False)


def share(value, axes, count):
    copies = jnp.broadcast_to(value[None], (count,) + value.shape)
    return swap(copies, axes).reshape(-1, value.shape[1])


VMEM = pl.BlockSpec(memory_space=pltpu.VMEM)
SMEM = pl.BlockSpec(memory_space=pltpu.SMEM)
HBM = pl.BlockSpec(memory_space=pltpu.MemorySpace.HBM)


def call(kernel, outs, flops, operands, in_specs=None, out_specs=None, scratch=(), limit=VMEM_BYTES):
    sizes = [a.size * a.dtype.itemsize for a in tuple(operands) + tuple(outs)]
    out = pl.pallas_call(
        kernel,
        out_shape=outs,
        in_specs=in_specs or [VMEM] * len(operands),
        out_specs=out_specs or [VMEM] * len(outs),
        scratch_shapes=scratch,
        compiler_params=pltpu.CompilerParams(vmem_limit_bytes=limit),
        cost_estimate=pl.CostEstimate(flops=flops, bytes_accessed=sum(sizes), transcendentals=0),
    )(*operands)
    return out[0] if len(outs) == 1 else out


def dispatch_kernel(capacity, routes_hbm, rows_hbm, out_hbm, routes_ref, rows_ref, out_ref, in_sem, out_sem):
    top, tokens = routes_ref.shape
    count = tokens * top
    experts = out_ref.shape[0] // capacity
    names = pltpu.make_async_copy(routes_hbm, routes_ref, in_sem.at[0])
    names.start()
    fetch = pltpu.make_async_copy(rows_hbm, rows_ref, in_sem.at[1])
    fetch.start()

    def iota(dims, axis):
        return lax.broadcasted_iota(jnp.int32, dims, axis)

    def flag(condition):
        return jnp.where(condition, 1.0, 0.0).astype(BF16)

    spread = flag(iota((top, count), 0) == iota((top, count), 1) % top)
    token = flag(iota((tokens, count), 0) == iota((tokens, count), 1) // top)
    earlier = flag(iota((count, count), 0) < iota((count, count), 1))
    names.wait()
    spelled = contract(routes_ref[...].astype(F32).astype(BF16), spread, 0, 0)
    expert = jnp.sum(spelled * token.astype(F32), axis=0, keepdims=True).astype(jnp.int32)
    named = flag(iota((experts, count), 0) == expert)
    before = jnp.dot(named, earlier, preferred_element_type=F32)
    position = jnp.sum(before * named.astype(F32), axis=0, keepdims=True)
    slot = expert * capacity + position.astype(jnp.int32)

    block = 256
    fetch.wait()
    rows = rows_ref[...]
    sends = []
    for i in range(out_ref.shape[0] // block):
        part = pl.ds(i * block, block)
        pick = flag(iota((block, count), 0) + i * block == slot)
        out_ref[part, :] = jnp.dot(pick, rows, preferred_element_type=F32).astype(BF16)
        sends.append(pltpu.make_async_copy(out_ref.at[part, :], out_hbm.at[part, :], out_sem.at[i]))
        sends[-1].start()
    for send in sends:
        send.wait()


def probe_kernel(quarter_ref, weight_ref, probe_ref, kept_ref, given_ref):
    quarter = quarter_ref[0]
    size = kept_ref.shape[0]
    probe = probe_ref[...]
    for step in (3, 2, 1, 0):
        start = pl.multiple_of((quarter ^ step) * size, size)
        part = contract(weight_ref[:, pl.ds(start, size)], probe, 0, 0)
        if step == 0:
            kept_ref[...] = part
        else:
            given_ref[step - 1] = part.astype(BF16)


def gram_kernel(quarter_ref, rows_ref, proj3, proj2, proj1, proj0, out_ref, proj_ref):
    quarter = quarter_ref[0]
    block = 256
    count, width = rows_ref.shape
    size = out_ref.shape[2]
    depth = proj0.shape[0]
    for step, part in enumerate((proj0, proj1, proj2, proj3)):
        proj_ref[pl.ds(pl.multiple_of((quarter ^ step) * depth, depth), depth), :] = part[...]
    proj = proj_ref[...]
    turned = []
    for i in range(count // block):
        mixed = jnp.dot(rows_ref[i * block : (i + 1) * block, :], proj, preferred_element_type=F32)
        turned.append(mixed.astype(BF16).T)
    turned = jnp.concatenate(turned, axis=1)
    for i in range(0, width, block):
        part = jnp.dot(turned, rows_ref[:, i : i + block], preferred_element_type=F32).astype(BF16)
        for j in range(0, block, size):
            out_ref[(i + j) // size] = part[:, j : j + size]


def share_kernel(scale, parts_ref, out_ref):
    cores, devices, _, half = out_ref.shape
    total = jnp.sum(parts_ref[...].astype(F32), axis=0) * scale
    value = total.astype(BF16).T
    for core in range(cores):
        for device in range(devices):
            out_ref[core, device] = value[:, core * half : (core + 1) * half]


def image_kernel(core_ref, own_ref, other_hbm, gram_ref, out_ref, other_ref, sems):
    core = core_ref[0]
    block = own_ref.shape[0] // sems.shape[0]
    parts = [pl.ds(i * block, block) for i in range(sems.shape[0])]
    fetches = [
        pltpu.make_async_copy(other_hbm.at[part, :], other_ref.at[part, :], sems.at[i]) for i, part in enumerate(parts)
    ]
    for fetch in fetches:
        fetch.start()
    own, other = gram_ref[core], gram_ref[1 - core]
    for part, fetch in zip(parts, fetches):
        image = jnp.dot(own_ref[part, :], own, preferred_element_type=F32)
        fetch.wait()
        image += jnp.dot(other_ref[part, :], other, preferred_element_type=F32)
        out_ref[part, :] = image.astype(BF16)


def coef_kernel(core_ref, own_ref, other_hbm, basis_ref, out_hbm, other_ref, out_ref, in_sems, out_sems):
    core = core_ref[0]
    size = out_ref.shape[3]
    block = own_ref.shape[1] // in_sems.shape[0]
    parts = [pl.ds(i * block, block) for i in range(in_sems.shape[0])]
    fetches = [
        pltpu.make_async_copy(other_hbm.at[:, part], other_ref.at[:, part], in_sems.at[i])
        for i, part in enumerate(parts)
    ]
    for fetch in fetches:
        fetch.start()
    turned = basis_ref[...].T
    sends = []
    for turn, (which, weight_ref) in enumerate(((core, own_ref), (1 - core, other_ref))):
        for i, part in enumerate(parts):
            if turn == 1:
                fetches[i].wait()
            value = jnp.dot(turned, weight_ref[:, part], preferred_element_type=F32).astype(BF16)
            for j in range(block // size):
                out_ref[turn, i * (block // size) + j] = value[:, j * size : (j + 1) * size]
        sends.append(pltpu.make_async_copy(out_ref.at[turn], out_hbm.at[which], out_sems.at[turn]))
        sends[-1].start()
    for send in sends:
        send.wait()


def total_kernel(parts_ref, out_ref):
    size = parts_ref.shape[2]
    for core in range(parts_ref.shape[0]):
        out_ref[core * size : (core + 1) * size, :] = jnp.sum(parts_ref[core].astype(F32), axis=0)


def body(hidden_rows, routes, down_weight, probe):
    weight = down_weight[0]
    tokens, top, width = hidden_rows.shape
    nx, ny, nc, nz = (lax.axis_size(a) for a in ("x", "y", "c", "z"))
    experts = nx * ny * nc
    chips = nx * ny
    capacity = 2 * tokens * top // experts
    row_mean = tokens * top * nz
    depth, panel = probe.shape
    half = panel // nc
    block = width // nz
    count = tokens * top
    core = lax.axis_index("c")
    me = lax.axis_index("z")

    def across(value, axis, size, step):
        return lax.ppermute(value, axis, [(i, i ^ step) for i in range(size)])

    def shape(dims, dtype):
        return jax.ShapeDtypeStruct(dims, dtype)

    slots = experts * capacity
    outgoing = call(
        functools.partial(dispatch_kernel, capacity),
        [shape((slots, width), BF16)],
        2 * slots * count * width,
        [routes.T, hidden_rows.reshape(count, width)],
        [HBM, HBM],
        [HBM],
        [
            pltpu.VMEM((top, tokens), jnp.int32),
            pltpu.VMEM((count, width), BF16),
            pltpu.VMEM((slots, width), BF16),
            pltpu.SemaphoreType.DMA((2,)),
            pltpu.SemaphoreType.DMA((slots // 256,)),
        ],
        WIDE_BYTES,
    )
    rows = swap(outgoing.reshape(experts, capacity, width), ("x", "y", "c")).reshape(slots, width)

    quarter = (me % 4)[None]
    four = width // 4
    kept, given = call(
        probe_kernel,
        [shape((four, panel), F32), shape((3, four, panel), BF16)],
        2 * depth * width * panel,
        [quarter, weight, probe],
        [SMEM, VMEM, VMEM],
    )
    proj = kept + sum(across(given[step - 1], "z", nz, step).astype(F32) for step in (1, 2, 3))
    proj = (proj + across(proj.astype(BF16), "z", nz, 4).astype(F32)).astype(BF16)
    quarters = [across(proj, "z", nz, step) for step in (1, 2, 3)]
    neighbour = across(weight, "c", nc, 1)

    rows, neighbour, core = lax.optimization_barrier((rows, neighbour, core))

    gram_part = call(
        gram_kernel,
        [shape((nz, panel, block), BF16)],
        4 * slots * width * panel,
        [quarter, rows] + quarters[::-1] + [proj],
        [SMEM] + [VMEM] * 5,
        None,
        [pltpu.VMEM((width, panel), BF16)],
    )
    copies = call(
        functools.partial(share_kernel, 1.0 / row_mean),
        [shape((nc, nz, block, half), BF16)],
        nz * block * panel,
        [swap(gram_part, "z")],
    )
    gram = swap(copies.reshape(nc * nz, block, half), ("c", "z")).reshape(nc, width, half)

    image = call(
        image_kernel,
        [shape((depth, half), BF16)],
        2 * depth * width * panel,
        [core[None], weight, neighbour, gram],
        [SMEM, VMEM, HBM, VMEM],
        None,
        [pltpu.VMEM((depth, width), BF16), pltpu.SemaphoreType.DMA((4,))],
    )
    pieces = swap(image.reshape(chips, depth // chips, half), ("x", "y"))
    own = jnp.sum(pieces.astype(F32), axis=0)
    basis = share(own.astype(BF16), ("x", "y"), chips)

    rows_own = depth // experts
    mine = lax.dynamic_slice_in_dim(own, core * rows_own, rows_own, 0)
    other = across(lax.dynamic_slice_in_dim(own, (1 - core) * rows_own, rows_own, 0), "c", nc, 1)
    basis_rows = jnp.where(core == 0, jnp.concatenate([mine, other], 1), jnp.concatenate([other, mine], 1))

    coef_part = call(
        coef_kernel,
        [shape((nc, nz, half, block), BF16)],
        2 * depth * width * panel,
        [core[None], weight, neighbour, basis],
        [SMEM, VMEM, HBM, VMEM],
        [HBM],
        [
            pltpu.VMEM((depth, width), BF16),
            pltpu.VMEM((nc, nz, half, block), BF16),
            pltpu.SemaphoreType.DMA((4,)),
            pltpu.SemaphoreType.DMA((nc,)),
        ],
    )
    arrived = swap(coef_part.reshape(nc * nz, half, block), ("c", "z")).reshape(nc, nz, half, block)
    coefficients = call(total_kernel, [shape((panel, block), F32)], nz * block * panel, [arrived])
    return basis_rows, coefficients[None]


def solution(mesh):
    grid = Mesh(mesh.devices.reshape(4, 8, 2, 8), ("x", "y", "c", "z"))
    expert = ("x", "y", "c")
    in_specs = (
        P(expert + ("z",), None, None),
        P(expert + ("z",), None),
        P(expert, "z", None),
        P("z", None),
    )
    out_specs = (P(("z",) + expert, None), P(expert, None, "z"))
    return jax.shard_map(body, mesh=grid, in_specs=in_specs, out_specs=out_specs, check_vma=False)
```

```python
import functools

import jax
import jax.numpy as jnp
from jax import lax
from jax.experimental import pallas as pl
from jax.experimental.pallas import tpu as pltpu
from jax.sharding import Mesh, PartitionSpec as P

F32 = jnp.float32
BF16 = jnp.bfloat16
VMEM_BYTES = 16 * 1024 * 1024
WIDE_BYTES = 125 * 512 * 1024


def contract(a, b, ca, cb):
    return lax.dot_general(a, b, (((ca,), (cb,)), ((), ())), preferred_element_type=F32)


def swap(value, axes):
    return lax.all_to_all(value, axes, split_axis=0, concat_axis=0, tiled=False)


def share(value, axes, count):
    copies = jnp.broadcast_to(value[None], (count,) + value.shape)
    return swap(copies, axes).reshape(-1, value.shape[1])


VMEM = pl.BlockSpec(memory_space=pltpu.VMEM)
SMEM = pl.BlockSpec(memory_space=pltpu.SMEM)
HBM = pl.BlockSpec(memory_space=pltpu.MemorySpace.HBM)


def call(kernel, outs, flops, operands, in_specs=None, out_specs=None, scratch=(), limit=VMEM_BYTES):
    sizes = [a.size * a.dtype.itemsize for a in tuple(operands) + tuple(outs)]
    out = pl.pallas_call(
        kernel,
        out_shape=outs,
        in_specs=in_specs or [VMEM] * len(operands),
        out_specs=out_specs or [VMEM] * len(outs),
        scratch_shapes=scratch,
        compiler_params=pltpu.CompilerParams(vmem_limit_bytes=limit),
        cost_estimate=pl.CostEstimate(flops=flops, bytes_accessed=sum(sizes), transcendentals=0),
    )(*operands)
    return out[0] if len(outs) == 1 else out


def dispatch_kernel(capacity, routes_hbm, rows_hbm, out_hbm, routes_ref, rows_ref, out_ref, in_sem, out_sem):
    top, tokens = routes_ref.shape
    count = tokens * top
    experts = out_ref.shape[0] // capacity
    names = pltpu.make_async_copy(routes_hbm, routes_ref, in_sem.at[0])
    names.start()
    fetch = pltpu.make_async_copy(rows_hbm, rows_ref, in_sem.at[1])
    fetch.start()

    def iota(dims, axis):
        return lax.broadcasted_iota(jnp.int32, dims, axis)

    def flag(condition):
        return jnp.where(condition, 1.0, 0.0).astype(BF16)

    spread = flag(iota((top, count), 0) == iota((top, count), 1) % top)
    token = flag(iota((tokens, count), 0) == iota((tokens, count), 1) // top)
    earlier = flag(iota((count, count), 0) < iota((count, count), 1))
    names.wait()
    spelled = contract(routes_ref[...].astype(F32).astype(BF16), spread, 0, 0)
    expert = jnp.sum(spelled * token.astype(F32), axis=0, keepdims=True).astype(jnp.int32)
    named = flag(iota((experts, count), 0) == expert)
    before = jnp.dot(named, earlier, preferred_element_type=F32)
    position = jnp.sum(before * named.astype(F32), axis=0, keepdims=True)
    slot = expert * capacity + position.astype(jnp.int32)

    block = 256
    fetch.wait()
    rows = rows_ref[...]
    sends = []
    for i in range(out_ref.shape[0] // block):
        part = pl.ds(i * block, block)
        pick = flag(iota((block, count), 0) + i * block == slot)
        out_ref[part, :] = jnp.dot(pick, rows, preferred_element_type=F32).astype(BF16)
        sends.append(pltpu.make_async_copy(out_ref.at[part, :], out_hbm.at[part, :], out_sem.at[i]))
        sends[-1].start()
    for send in sends:
        send.wait()


def probe_kernel(quarter_ref, weight_ref, probe_ref, kept_ref, given_ref):
    quarter = quarter_ref[0]
    size = kept_ref.shape[0]
    probe = probe_ref[...]
    for step in (3, 2, 1, 0):
        start = pl.multiple_of((quarter ^ step) * size, size)
        part = contract(weight_ref[:, pl.ds(start, size)], probe, 0, 0)
        if step == 0:
            kept_ref[...] = part
        else:
            given_ref[step - 1] = part.astype(BF16)


def gram_kernel(quarter_ref, rows_ref, proj3, proj2, proj1, proj0, out_ref, proj_ref):
    quarter = quarter_ref[0]
    block = 256
    count, width = rows_ref.shape
    size = out_ref.shape[3]
    half = out_ref.shape[2]
    depth = proj0.shape[0]
    for step, part in enumerate((proj0, proj1, proj2, proj3)):
        proj_ref[pl.ds(pl.multiple_of((quarter ^ step) * depth, depth), depth), :] = part[...]
    proj = proj_ref[...]
    turned = []
    for i in range(count // block):
        mixed = jnp.dot(rows_ref[i * block : (i + 1) * block, :], proj, preferred_element_type=F32)
        turned.append(mixed.astype(BF16).T)
    turned = jnp.concatenate(turned, axis=1)
    for i in range(0, width, block):
        part = jnp.dot(turned, rows_ref[:, i : i + block], preferred_element_type=F32).astype(BF16)
        for j in range(0, block, size):
            for core in range(out_ref.shape[0]):
                out_ref[core, (i + j) // size] = part[core * half : (core + 1) * half, j : j + size]


def share_kernel(scale, parts_ref, out_ref):
    for expert in range(parts_ref.shape[0]):
        total = jnp.sum(parts_ref[expert].astype(F32), axis=0) * scale
        value = total.astype(BF16).T
        for device in range(out_ref.shape[0]):
            out_ref[device, expert] = value


def image_kernel(core_ref, own_ref, other_hbm, gram_ref, out_ref, other_ref, sems):
    core = core_ref[0]
    block = own_ref.shape[0] // sems.shape[0]
    parts = [pl.ds(i * block, block) for i in range(sems.shape[0])]
    fetches = [
        pltpu.make_async_copy(other_hbm.at[part, :], other_ref.at[part, :], sems.at[i]) for i, part in enumerate(parts)
    ]
    for fetch in fetches:
        fetch.start()
    own, other = (gram_ref[:, i].reshape(-1, gram_ref.shape[3]) for i in (core, 1 - core))
    for part, fetch in zip(parts, fetches):
        image = jnp.dot(own_ref[part, :], own, preferred_element_type=F32)
        fetch.wait()
        image += jnp.dot(other_ref[part, :], other, preferred_element_type=F32)
        out_ref[part, :] = image.astype(BF16)


def coef_kernel(core_ref, own_ref, other_hbm, basis_ref, out_hbm, other_ref, out_ref, in_sems, out_sems):
    core = core_ref[0]
    size = out_ref.shape[3]
    block = own_ref.shape[1] // in_sems.shape[0]
    parts = [pl.ds(i * block, block) for i in range(in_sems.shape[0])]
    fetches = [
        pltpu.make_async_copy(other_hbm.at[:, part], other_ref.at[:, part], in_sems.at[i])
        for i, part in enumerate(parts)
    ]
    for fetch in fetches:
        fetch.start()
    turned = basis_ref[...].T
    sends = []
    for turn, (which, weight_ref) in enumerate(((core, own_ref), (1 - core, other_ref))):
        for i, part in enumerate(parts):
            if turn == 1:
                fetches[i].wait()
            value = jnp.dot(turned, weight_ref[:, part], preferred_element_type=F32).astype(BF16)
            for j in range(block // size):
                out_ref[turn, i * (block // size) + j] = value[:, j * size : (j + 1) * size]
        sends.append(pltpu.make_async_copy(out_ref.at[turn], out_hbm.at[which], out_sems.at[turn]))
        sends[-1].start()
    for send in sends:
        send.wait()


def total_kernel(parts_ref, out_ref):
    size = parts_ref.shape[2]
    for core in range(parts_ref.shape[0]):
        out_ref[core * size : (core + 1) * size, :] = jnp.sum(parts_ref[core].astype(F32), axis=0)


def body(hidden_rows, routes, down_weight, probe):
    weight = down_weight[0]
    tokens, top, width = hidden_rows.shape
    nx, ny, nc, nz = (lax.axis_size(a) for a in ("x", "y", "c", "z"))
    experts = nx * ny * nc
    chips = nx * ny
    capacity = 2 * tokens * top // experts
    row_mean = tokens * top * nz
    depth, panel = probe.shape
    half = panel // nc
    block = width // nz
    count = tokens * top
    core = lax.axis_index("c")
    me = lax.axis_index("z")

    def across(value, axis, size, step):
        return lax.ppermute(value, axis, [(i, i ^ step) for i in range(size)])

    def shape(dims, dtype):
        return jax.ShapeDtypeStruct(dims, dtype)

    slots = experts * capacity
    outgoing = call(
        functools.partial(dispatch_kernel, capacity),
        [shape((slots, width), BF16)],
        2 * slots * count * width,
        [routes.T, hidden_rows.reshape(count, width)],
        [HBM, HBM],
        [HBM],
        [
            pltpu.VMEM((top, tokens), jnp.int32),
            pltpu.VMEM((count, width), BF16),
            pltpu.VMEM((slots, width), BF16),
            pltpu.SemaphoreType.DMA((2,)),
            pltpu.SemaphoreType.DMA((slots // 256,)),
        ],
        WIDE_BYTES,
    )
    rows = swap(outgoing.reshape(experts, capacity, width), ("x", "y", "c")).reshape(slots, width)

    quarter = (me % 4)[None]
    four = width // 4
    kept, given = call(
        probe_kernel,
        [shape((four, panel), F32), shape((3, four, panel), BF16)],
        2 * depth * width * panel,
        [quarter, weight, probe],
        [SMEM, VMEM, VMEM],
    )
    proj = kept + sum(across(given[step - 1], "z", nz, step).astype(F32) for step in (1, 2, 3))
    proj = (proj + across(proj.astype(BF16), "z", nz, 4).astype(F32)).astype(BF16)
    quarters = [across(proj, "z", nz, step) for step in (1, 2, 3)]
    neighbour = across(weight, "c", nc, 1)

    rows, neighbour, core = lax.optimization_barrier((rows, neighbour, core))

    gram_part = call(
        gram_kernel,
        [shape((nc, nz, half, block), BF16)],
        4 * slots * width * panel,
        [quarter, rows] + quarters[::-1] + [proj],
        [SMEM] + [VMEM] * 5,
        None,
        [pltpu.VMEM((width, panel), BF16)],
    )
    arrived = swap(gram_part.reshape(nc * nz, half, block), ("c", "z")).reshape(nc, nz, half, block)
    copies = call(
        functools.partial(share_kernel, 1.0 / row_mean),
        [shape((nz, nc, block, half), BF16)],
        nz * block * panel,
        [arrived],
    )
    gram = swap(copies, "z")

    image = call(
        image_kernel,
        [shape((depth, half), BF16)],
        2 * depth * width * panel,
        [core[None], weight, neighbour, gram],
        [SMEM, VMEM, HBM, VMEM],
        None,
        [pltpu.VMEM((depth, width), BF16), pltpu.SemaphoreType.DMA((4,))],
    )
    pieces = swap(image.reshape(chips, depth // chips, half), ("x", "y"))
    own = jnp.sum(pieces.astype(F32), axis=0)
    basis = share(own.astype(BF16), ("x", "y"), chips)

    rows_own = depth // experts
    mine = lax.dynamic_slice_in_dim(own, core * rows_own, rows_own, 0)
    other = across(lax.dynamic_slice_in_dim(own, (1 - core) * rows_own, rows_own, 0), "c", nc, 1)
    basis_rows = jnp.where(core == 0, jnp.concatenate([mine, other], 1), jnp.concatenate([other, mine], 1))

    coef_part = call(
        coef_kernel,
        [shape((nc, nz, half, block), BF16)],
        2 * depth * width * panel,
        [core[None], weight, neighbour, basis],
        [SMEM, VMEM, HBM, VMEM],
        [HBM],
        [
            pltpu.VMEM((depth, width), BF16),
            pltpu.VMEM((nc, nz, half, block), BF16),
            pltpu.SemaphoreType.DMA((4,)),
            pltpu.SemaphoreType.DMA((nc,)),
        ],
    )
    arrived = swap(coef_part.reshape(nc * nz, half, block), ("c", "z")).reshape(nc, nz, half, block)
    coefficients = call(total_kernel, [shape((panel, block), F32)], nz * block * panel, [arrived])
    return basis_rows, coefficients[None]


def solution(mesh):
    grid = Mesh(mesh.devices.reshape(4, 8, 2, 8), ("x", "y", "c", "z"))
    expert = ("x", "y", "c")
    in_specs = (
        P(expert + ("z",), None, None),
        P(expert + ("z",), None),
        P(expert, "z", None),
        P("z", None),
    )
    out_specs = (P(("z",) + expert, None), P(expert, None, "z"))
    return jax.shard_map(body, mesh=grid, in_specs=in_specs, out_specs=out_specs, check_vma=False)
```

```python
import functools

import jax
import jax.numpy as jnp
from jax import lax
from jax.experimental import pallas as pl
from jax.experimental.pallas import tpu as pltpu
from jax.sharding import Mesh, PartitionSpec as P

F32 = jnp.float32
BF16 = jnp.bfloat16
VMEM_BYTES = 16 * 1024 * 1024
WIDE_BYTES = 125 * 512 * 1024


def contract(a, b, ca, cb):
    return lax.dot_general(a, b, (((ca,), (cb,)), ((), ())), preferred_element_type=F32)


def swap(value, axes):
    return lax.all_to_all(value, axes, split_axis=0, concat_axis=0, tiled=False)


VMEM = pl.BlockSpec(memory_space=pltpu.VMEM)
SMEM = pl.BlockSpec(memory_space=pltpu.SMEM)
HBM = pl.BlockSpec(memory_space=pltpu.MemorySpace.HBM)


def call(kernel, outs, flops, operands, in_specs=None, out_specs=None, scratch=(), limit=VMEM_BYTES):
    sizes = [a.size * a.dtype.itemsize for a in tuple(operands) + tuple(outs)]
    out = pl.pallas_call(
        kernel,
        out_shape=outs,
        in_specs=in_specs or [VMEM] * len(operands),
        out_specs=out_specs or [VMEM] * len(outs),
        scratch_shapes=scratch,
        compiler_params=pltpu.CompilerParams(vmem_limit_bytes=limit),
        cost_estimate=pl.CostEstimate(flops=flops, bytes_accessed=sum(sizes), transcendentals=0),
    )(*operands)
    return out[0] if len(outs) == 1 else out


def dispatch_kernel(capacity, routes_hbm, rows_hbm, out_hbm, routes_ref, rows_ref, out_ref, in_sem, out_sem):
    top, tokens = routes_ref.shape
    count = tokens * top
    experts = out_ref.shape[0] // capacity
    names = pltpu.make_async_copy(routes_hbm, routes_ref, in_sem.at[0])
    names.start()
    fetch = pltpu.make_async_copy(rows_hbm, rows_ref, in_sem.at[1])
    fetch.start()

    def iota(dims, axis):
        return lax.broadcasted_iota(jnp.int32, dims, axis)

    def flag(condition):
        return jnp.where(condition, 1.0, 0.0).astype(BF16)

    spread = flag(iota((top, count), 0) == iota((top, count), 1) % top)
    token = flag(iota((tokens, count), 0) == iota((tokens, count), 1) // top)
    earlier = flag(iota((count, count), 0) < iota((count, count), 1))
    names.wait()
    spelled = contract(routes_ref[...].astype(F32).astype(BF16), spread, 0, 0)
    expert = jnp.sum(spelled * token.astype(F32), axis=0, keepdims=True).astype(jnp.int32)
    named = flag(iota((experts, count), 0) == expert)
    before = jnp.dot(named, earlier, preferred_element_type=F32)
    position = jnp.sum(before * named.astype(F32), axis=0, keepdims=True)
    slot = expert * capacity + position.astype(jnp.int32)

    block = 256
    fetch.wait()
    rows = rows_ref[...]
    sends = []
    for i in range(out_ref.shape[0] // block):
        part = pl.ds(i * block, block)
        pick = flag(iota((block, count), 0) + i * block == slot)
        out_ref[part, :] = jnp.dot(pick, rows, preferred_element_type=F32).astype(BF16)
        sends.append(pltpu.make_async_copy(out_ref.at[part, :], out_hbm.at[part, :], out_sem.at[i]))
        sends[-1].start()
    for send in sends:
        send.wait()


def probe_kernel(quarter_ref, weight_ref, probe_ref, kept_ref, given_ref):
    quarter = quarter_ref[0]
    size = kept_ref.shape[0]
    probe = probe_ref[...]
    for step in (3, 2, 1, 0):
        start = pl.multiple_of((quarter ^ step) * size, size)
        part = contract(weight_ref[:, pl.ds(start, size)], probe, 0, 0)
        if step == 0:
            kept_ref[...] = part
        else:
            given_ref[step - 1] = part.astype(BF16)


def gram_kernel(quarter_ref, rows_ref, proj3, proj2, proj1, proj0, out_ref, proj_ref):
    quarter = quarter_ref[0]
    block = 256
    count, width = rows_ref.shape
    size = out_ref.shape[3]
    half = out_ref.shape[2]
    depth = proj0.shape[0]
    for step, part in enumerate((proj0, proj1, proj2, proj3)):
        proj_ref[pl.ds(pl.multiple_of((quarter ^ step) * depth, depth), depth), :] = part[...]
    proj = proj_ref[...]
    turned = []
    for i in range(count // block):
        mixed = jnp.dot(rows_ref[i * block : (i + 1) * block, :], proj, preferred_element_type=F32)
        turned.append(mixed.astype(BF16).T)
    turned = jnp.concatenate(turned, axis=1)
    for i in range(0, width, block):
        part = jnp.dot(turned, rows_ref[:, i : i + block], preferred_element_type=F32).astype(BF16)
        for j in range(0, block, size):
            for core in range(out_ref.shape[0]):
                out_ref[core, (i + j) // size] = part[core * half : (core + 1) * half, j : j + size]


def share_kernel(scale, parts_ref, out_ref):
    for expert in range(parts_ref.shape[0]):
        total = jnp.sum(parts_ref[expert].astype(F32), axis=0) * scale
        value = total.astype(BF16).T
        for device in range(out_ref.shape[0]):
            out_ref[device, expert] = value


def image_kernel(core_ref, own_ref, other_hbm, gram_ref, out_ref, other_ref, sems):
    core = core_ref[0]
    block = own_ref.shape[0] // sems.shape[0]
    parts = [pl.ds(i * block, block) for i in range(sems.shape[0])]
    fetches = [
        pltpu.make_async_copy(other_hbm.at[part, :], other_ref.at[part, :], sems.at[i]) for i, part in enumerate(parts)
    ]
    for fetch in fetches:
        fetch.start()
    own, other = (gram_ref[:, i].reshape(-1, gram_ref.shape[3]) for i in (core, 1 - core))
    for part, fetch in zip(parts, fetches):
        image = jnp.dot(own_ref[part, :], own, preferred_element_type=F32)
        fetch.wait()
        image += jnp.dot(other_ref[part, :], other, preferred_element_type=F32)
        out_ref[part, :] = image.astype(BF16)


def coef_kernel(core_ref, own_ref, other_hbm, basis_ref, out_ref, other_ref, sems):
    core = core_ref[0]
    size = out_ref.shape[3]
    block = own_ref.shape[1] // sems.shape[0]
    parts = [pl.ds(i * block, block) for i in range(sems.shape[0])]
    fetches = [
        pltpu.make_async_copy(other_hbm.at[:, part], other_ref.at[:, part], sems.at[i])
        for i, part in enumerate(parts)
    ]
    for fetch in fetches:
        fetch.start()
    turned = basis_ref[...].T
    for turn, (which, weight_ref) in enumerate(((core, own_ref), (1 - core, other_ref))):
        for i, part in enumerate(parts):
            if turn == 1:
                fetches[i].wait()
            value = jnp.dot(turned, weight_ref[:, part], preferred_element_type=F32).astype(BF16)
            for j in range(block // size):
                out_ref[which, i * (block // size) + j] = value[:, j * size : (j + 1) * size]


def spread_kernel(pieces_ref, own_ref, copies_ref):
    own = jnp.sum(pieces_ref[...].astype(F32), axis=0)
    own_ref[...] = own
    value = own.astype(BF16)
    for i in range(copies_ref.shape[0]):
        copies_ref[i] = value


def total_kernel(parts_ref, out_ref):
    size = parts_ref.shape[2]
    for core in range(parts_ref.shape[0]):
        out_ref[core * size : (core + 1) * size, :] = jnp.sum(parts_ref[core].astype(F32), axis=0)


def body(hidden_rows, routes, down_weight, probe):
    weight = down_weight[0]
    tokens, top, width = hidden_rows.shape
    nx, ny, nc, nz = (lax.axis_size(a) for a in ("x", "y", "c", "z"))
    experts = nx * ny * nc
    chips = nx * ny
    capacity = 2 * tokens * top // experts
    row_mean = tokens * top * nz
    depth, panel = probe.shape
    half = panel // nc
    block = width // nz
    count = tokens * top
    core = lax.axis_index("c")
    me = lax.axis_index("z")

    def across(value, axis, size, step):
        return lax.ppermute(value, axis, [(i, i ^ step) for i in range(size)])

    def shape(dims, dtype):
        return jax.ShapeDtypeStruct(dims, dtype)

    slots = experts * capacity
    outgoing = call(
        functools.partial(dispatch_kernel, capacity),
        [shape((slots, width), BF16)],
        2 * slots * count * width,
        [routes.T, hidden_rows.reshape(count, width)],
        [HBM, HBM],
        [HBM],
        [
            pltpu.VMEM((top, tokens), jnp.int32),
            pltpu.VMEM((count, width), BF16),
            pltpu.VMEM((slots, width), BF16),
            pltpu.SemaphoreType.DMA((2,)),
            pltpu.SemaphoreType.DMA((slots // 256,)),
        ],
        WIDE_BYTES,
    )
    rows = swap(outgoing.reshape(experts, capacity, width), ("x", "y", "c")).reshape(slots, width)

    quarter = (me % 4)[None]
    four = width // 4
    kept, given = call(
        probe_kernel,
        [shape((four, panel), F32), shape((3, four, panel), BF16)],
        2 * depth * width * panel,
        [quarter, weight, probe],
        [SMEM, VMEM, VMEM],
    )
    proj = kept + sum(across(given[step - 1], "z", nz, step).astype(F32) for step in (1, 2, 3))
    proj = (proj + across(proj.astype(BF16), "z", nz, 4).astype(F32)).astype(BF16)
    quarters = [across(proj, "z", nz, step) for step in (1, 2, 3)]
    neighbour = across(weight, "c", nc, 1)

    rows, neighbour, core = lax.optimization_barrier((rows, neighbour, core))

    gram_part = call(
        gram_kernel,
        [shape((nc, nz, half, block), BF16)],
        4 * slots * width * panel,
        [quarter, rows] + quarters[::-1] + [proj],
        [SMEM] + [VMEM] * 5,
        None,
        [pltpu.VMEM((width, panel), BF16)],
    )
    arrived = swap(gram_part.reshape(nc * nz, half, block), ("c", "z")).reshape(nc, nz, half, block)
    copies = call(
        functools.partial(share_kernel, 1.0 / row_mean),
        [shape((nz, nc, block, half), BF16)],
        nz * block * panel,
        [arrived],
    )
    gram = swap(copies, "z")

    image = call(
        image_kernel,
        [shape((depth, half), BF16)],
        2 * depth * width * panel,
        [core[None], weight, neighbour, gram],
        [SMEM, VMEM, HBM, VMEM],
        None,
        [pltpu.VMEM((depth, width), BF16), pltpu.SemaphoreType.DMA((4,))],
    )
    pieces = swap(image.reshape(chips, depth // chips, half), ("x", "y"))
    own, copies = call(
        spread_kernel,
        [shape((depth // chips, half), F32), shape(pieces.shape, BF16)],
        depth * half,
        [pieces],
    )
    basis = swap(copies, ("x", "y")).reshape(depth, half)

    rows_own = depth // experts
    mine = lax.dynamic_slice_in_dim(own, core * rows_own, rows_own, 0)
    other = across(lax.dynamic_slice_in_dim(own, (1 - core) * rows_own, rows_own, 0), "c", nc, 1)
    basis_rows = jnp.where(core == 0, jnp.concatenate([mine, other], 1), jnp.concatenate([other, mine], 1))

    basis, basis_rows = lax.optimization_barrier((basis, basis_rows))

    coef_part = call(
        coef_kernel,
        [shape((nc, nz, half, block), BF16)],
        2 * depth * width * panel,
        [core[None], weight, neighbour, basis],
        [SMEM, VMEM, HBM, VMEM],
        None,
        [pltpu.VMEM((depth, width), BF16), pltpu.SemaphoreType.DMA((4,))],
    )
    arrived = swap(coef_part.reshape(nc * nz, half, block), ("c", "z")).reshape(nc, nz, half, block)
    coefficients = call(total_kernel, [shape((panel, block), F32)], nz * block * panel, [arrived])
    return basis_rows, coefficients[None]


def solution(mesh):
    grid = Mesh(mesh.devices.reshape(4, 8, 2, 8), ("x", "y", "c", "z"))
    expert = ("x", "y", "c")
    in_specs = (
        P(expert + ("z",), None, None),
        P(expert + ("z",), None),
        P(expert, "z", None),
        P("z", None),
    )
    out_specs = (P(("z",) + expert, None), P(expert, None, "z"))
    return jax.shard_map(body, mesh=grid, in_specs=in_specs, out_specs=out_specs, check_vma=False)
```
